32 devices in a mesh: row: 4 (over y, x), col: 8 (over z, core).
Axes of the slice: x: 2, y: 2, z: 4, core: 2. Of those that a mesh axis runs over, the one named last changes fastest.
Arguments:
- preference: bfloat16 [8192, 16384], P('col', 'row'), may hold values from -6 to 6
- users: float32 [64, 16384], P(None, 'row'), may hold values from -2 to 2
- items: float32 [64, 8192], P(None, ('col', 'row')), may hold values from -2 to 2
Outputs:
- new_users: float32 [64, 16384], P(None, 'row')
- new_items: float32 [64, 8192], P(None, ('col', 'row'))
The draws below stay inside these ranges and needn't reach their ends.
All inputs are finite; a program needn't handle non-finite values.
Results may differ from the reference program's by a relative error of at most 0.0051.
Values may be sent and summed in bfloat16 or wider, within the bound.
No kernel may reach another device: no remote copies, remote signals or barrier semaphores. Data moves between devices by JAX's collectives and lax.ppermute only.
A program may use at most 64 MiB of HBM per device.

```python
import math
import jax
import jax.numpy as jnp
from jax import lax

RANK = 64
ITEMS_DEV = 1024
ITERS = 2
USERS = 16384
ITEMS = 8192


def block_levels(stream_key, extent, split, low, high):
    def one(position, shards_of):
        draws = jax.random.uniform(jax.random.fold_in(jax.random.fold_in(stream_key, 6), position), (shards_of,), jnp.float32, low / len(split), high / len(split))
        return jnp.repeat(jnp.exp(draws), extent[position] // shards_of).reshape((-1,) + (1,) * (len(extent) - position - 1))

    gain = one(*split[0])
    for cut in split[1:]:
        gain = gain * one(*cut)
    return gain


def gaussian(key, dims, deviation, most, cuts=(), kind=jnp.bfloat16):
    result = jax.random.normal(key, dims, jnp.float32) * deviation
    if len(cuts) > 0:
        result = block_levels(key, dims, cuts, -0.22, 0.18) * result
    return jnp.clip(result, min=-most, max=most).astype(kind)


def setup_inputs(seed: int = 0) -> dict:
    splits = jax.random.split(jax.random.key(seed), 4)
    preference = gaussian(splits[0], (ITEMS, USERS), 1.0, 6.0, ((0, 8), (1, 4)))
    users = gaussian(splits[1], (RANK, USERS), 0.35, 2.0, ((1, 4),), jnp.float32)
    items = gaussian(splits[2], (RANK, ITEMS), 0.35, 2.0, ((1, 32),), jnp.float32)
    return dict(preference=preference, users=users, items=items)


step_scale = 1.0

def reference(preference, users, items):
    item_count, user_count = preference.shape
    user_rate = step_scale / math.sqrt(item_count)
    item_rate = step_scale / math.sqrt(user_count)
    block_count = item_count // ITEMS_DEV
    labels_blocks = preference.reshape(block_count, ITEMS_DEV, user_count)
    for iteration in range(ITERS):
        user_b = users.astype(jnp.bfloat16).astype(jnp.float32)
        item_b = items.astype(jnp.bfloat16).astype(jnp.float32)
        item_blocks = item_b.reshape(RANK, block_count, ITEMS_DEV).transpose(1, 0, 2)

        def visit(running, pair_block):
            labels_block, factor_block = pair_block
            scores = jnp.einsum('kn,km->nm', factor_block, user_b)
            weights = labels_block.astype(jnp.float32)
            residual = jnp.abs(weights) * jax.nn.sigmoid(scores) - jnp.maximum(weights, 0.0)
            residual = residual.astype(jnp.bfloat16).astype(jnp.float32)
            running = running + jnp.einsum('kn,nm->km', factor_block, residual)
            return (running, jnp.einsum('km,nm->kn', user_b, residual))
        grad_user, grad_blocks = lax.scan(visit, jnp.zeros((RANK, user_count), jnp.float32), (labels_blocks, item_blocks))
        grad_item = grad_blocks.transpose(1, 0, 2).reshape(RANK, item_count)
        users = users - user_rate * grad_user
        items = items - item_rate * grad_item
    return (users, items)
```

```python
import functools
import math

import jax
import jax.numpy as jnp
from jax import lax
from jax.experimental import pallas as pl
from jax.experimental.pallas import tpu as pltpu
from jax.sharding import PartitionSpec as P

ITERS = 2
CORES = 2
TILE_USERS = 1024
TILE_ITEMS = 512

f32, bf16 = jnp.float32, jnp.bfloat16


def swap(block, axis, distance):
    return lax.ppermute(block, axis, [(i, i ^ distance) for i in range(lax.axis_size(axis))])


def tree_sum(terms):
    while len(terms) > 1:
        terms = [terms[i] + terms[i + 1] for i in range(0, len(terms), 2)]
    return terms[0]


def span(index, width):
    return pl.ds(pl.multiple_of(index * width, width), width)


def call(kernel, outs, *args, scratch=(), flops=0):
    whole = pl.BlockSpec(memory_space=pltpu.VMEM)
    moved = sum(a.size * a.dtype.itemsize for a in args)
    return pl.pallas_call(
        kernel,
        in_specs=[whole] * len(args),
        out_specs=[whole] * len(outs),
        out_shape=[jax.ShapeDtypeStruct(s, d) for s, d in outs],
        scratch_shapes=list(scratch),
        compiler_params=pltpu.CompilerParams(vmem_limit_bytes=24 << 20),
        cost_estimate=pl.CostEstimate(flops=flops, bytes_accessed=moved, transcendentals=0),
    )(*args)


def gradients(columns, user_of, item_ref, item_t_ref, labels_ref, grad_item_ref, keep):
    start, width = columns
    tile_users, tile_items = min(TILE_USERS, width), min(TILE_ITEMS, labels_ref.shape[0])
    for at in range(0, width, tile_users):
        here = pl.ds(pl.multiple_of(start + at, tile_users), tile_users)
        user = user_of(at, tile_users)
        total = None
        for row in range(0, labels_ref.shape[0], tile_items):
            rows = pl.ds(row, tile_items)
            half_scores = jnp.dot(item_t_ref[rows, :], user, preferred_element_type=f32)
            weights = labels_ref[rows, here].astype(f32)
            residual = (jnp.abs(weights) * jnp.tanh(half_scores) - weights).astype(bf16)
            term = jnp.dot(item_ref[:, rows], residual, preferred_element_type=f32)
            total = term if total is None else total + term
            grad_item_ref[:, rows] += lax.dot_general(
                user, residual, (((1,), (1,)), ((), ())), preferred_element_type=f32
            )
        keep(at, tile_users, total)


def store_into(ref, offset=0):
    def keep(at, width, value):
        ref[:, pl.ds(offset + at, width)] = value.astype(ref.dtype)

    return keep


def put_items(item, item_ref, item_t_ref):
    rounded = item.astype(bf16)
    item_ref[...] = rounded
    item_t_ref[...] = (rounded * jnp.asarray(0.5, bf16)).T


def combine(keep_ref, recv_ref, share, own_ref, send_refs):
    z = lax.axis_index("col") // CORES
    for o in range(len(send_refs) + 1):
        at = span(z ^ o, share)
        piece = keep_ref[:, at] + recv_ref[:, at].astype(f32)
        if o == 0:
            own_ref[...] = piece
        else:
            send_refs[o - 1][...] = piece.astype(bf16)


def first_peer(rows_count, half, *refs):
    blocks, (users, labels) = refs[:rows_count], refs[rows_count : rows_count + 2]
    send, grad_item, item_all, item, item_t = refs[rows_count + 2 :]
    row, core = lax.axis_index("row"), lax.axis_index("col") % CORES
    for o, block in enumerate(blocks):
        item_all[:, span(row ^ o, block.shape[1])] = block[...]
    put_items(item_all[...], item, item_t)
    grad_item[...] = jnp.zeros_like(grad_item)
    start = (1 - core) * half

    def user_of(at, width):
        return users[:, pl.ds(pl.multiple_of(start + at, width), width)].astype(bf16)

    gradients((start, half), user_of, item, item_t, labels, grad_item, store_into(send))


def first_own(part, width, half, users, labels, item, item_t, grad_in, kept, grad_item):
    start = (lax.axis_index("col") % CORES) * half + part
    grad_item[...] = grad_in[...]

    def user_of(at, w):
        return users[:, pl.ds(pl.multiple_of(start + at, w), w)].astype(bf16)

    gradients((start, width), user_of, item, item_t, labels, grad_item, store_into(kept))


def first_last(part, width, half, share, chips, users, labels, item, item_t, grad_in, kept_in, recv, *refs):
    own, sends, grad_out = refs[0], refs[1:chips], refs[chips]
    kept, grad_item = refs[chips + 1 :]
    start = (lax.axis_index("col") % CORES) * half + part
    grad_item[...] = grad_in[...]
    kept[:, pl.ds(0, part)] = kept_in[...]

    def user_of(at, w):
        return users[:, pl.ds(pl.multiple_of(start + at, w), w)].astype(bf16)

    gradients((start, width), user_of, item, item_t, labels, grad_item, store_into(kept, part))
    grad_out[...] = grad_item[...].astype(bf16)
    combine(kept, recv, share, own, sends)


def share_at(half, share):
    col = lax.axis_index("col")
    return pl.ds(pl.multiple_of((col % CORES) * half + (col // CORES) * share, share), share)


def update_share(rate, half, share, own, *refs):
    recvs, (users, new, new_b) = refs[:-3], refs[-3:]
    grad = tree_sum([own[...]] + [r[...].astype(f32) for r in recvs])
    new[...] = users[:, share_at(half, share)] - rate * grad
    new_b[...] = new[...].astype(bf16)


def update_last(rate, half, share, own, *refs):
    recvs, (users, new, delta_b) = refs[:-3], refs[-3:]
    grad = tree_sum([own[...]] + [r[...].astype(f32) for r in recvs])
    delta_b[...] = (new[...] - rate * grad - users[:, share_at(half, share)]).astype(bf16)


def second_start(rate, rows_count, chips, *refs):
    grads, item_all = refs[:rows_count], refs[rows_count]
    pieces = refs[rows_count + 1 : rows_count + 1 + chips]
    item_own, item, item_t, user_half = refs[rows_count + 1 + chips :]
    assemble(pieces, user_half)
    new = item_all[...] - rate * tree_sum([g[...].astype(f32) for g in grads])
    put_items(new, item, item_t)
    block = item_own.shape[1]
    at = span(lax.axis_index("row"), block)
    grad = tree_sum([g[:, at].astype(f32) for g in grads])
    item_own[...] = item_all[:, at] - rate * grad


def assemble(pieces, user_half):
    z = lax.axis_index("col") // CORES
    for o, piece in enumerate(pieces):
        user_half[:, span(z ^ o, piece.shape[1])] = piece[...]


def second_own(part, width, half, user_half, labels, item, item_t, grad_in, kept, grad_item):
    start = (lax.axis_index("col") % CORES) * half + part
    if grad_in is None:
        grad_item[...] = jnp.zeros_like(grad_item)
    else:
        grad_item[...] = grad_in[...]

    def user_of(at, w):
        return user_half[:, pl.ds(part + at, w)]

    gradients((start, width), user_of, item, item_t, labels, grad_item, store_into(kept))


def second_open(part, width, half, user_half, labels, item, item_t, kept, grad_item):
    second_own(part, width, half, user_half, labels, item, item_t, None, kept, grad_item)


def second_peer(half, user_half, labels, item, item_t, grad_in, send, grad_item):
    start = (1 - lax.axis_index("col") % CORES) * half
    grad_item[...] = grad_in[...]

    def user_of(at, w):
        return user_half[:, pl.ds(at, w)]

    gradients((start, half), user_of, item, item_t, labels, grad_item, store_into(send))


def second_last(parts, half, share, chips, rows_count, user_half, labels, item, item_t, grad_in, kept0, kept1, recv, *refs):
    own, sends = refs[0], refs[1:chips]
    item_own, item_sends = refs[chips], refs[chips + 1 : chips + rows_count]
    kept, grad_item = refs[chips + rows_count :]
    first, second = parts
    start = (lax.axis_index("col") % CORES) * half
    grad_item[...] = grad_in[...]
    kept[:, pl.ds(0, first)] = kept0[...]
    kept[:, pl.ds(first, second)] = kept1[...]
    part = first + second

    def user_of(at, w):
        return user_half[:, pl.ds(part + at, w)]

    gradients((start + part, half - part), user_of, item, item_t, labels, grad_item, store_into(kept, part))
    combine(kept, recv, share, own, sends)
    row, block = lax.axis_index("row"), item_own.shape[1]
    for o in range(rows_count):
        piece = grad_item[:, span(row ^ o, block)]
        if o == 0:
            item_own[...] = piece
        else:
            item_sends[o - 1][...] = piece.astype(bf16)


def gather_half(chips, *refs):
    assemble(refs[:chips], refs[chips])


def finish_items(rate, item, own, *refs):
    recvs, out = refs[:-1], refs[-1]
    out[...] = item[...] - rate * tree_sum([own[...]] + [r[...].astype(f32) for r in recvs])


def finish_users(half, users, own, peer, out):
    core = lax.axis_index("col") % CORES
    mine, other = span(core, half), span(1 - core, half)
    out[:, mine] = users[:, mine] + own[...].astype(f32)
    out[:, other] = users[:, other] + peer[...].astype(f32)


def body(preference, users, items):
    rows_count, cols_count = lax.axis_size("row"), lax.axis_size("col")
    items_dev, users_dev = preference.shape
    rank, block = items.shape
    chips = cols_count // CORES
    half, share = users_dev // CORES, users_dev // cols_count
    user_rate = 0.5 / math.sqrt(items_dev * cols_count)
    item_rate = 0.5 / math.sqrt(users_dev * rows_count)
    work = lambda width: 6 * rank * items_dev * width
    grad_items = ((rank, items_dev), f32)
    item_pair = [((rank, items_dev), bf16), ((items_dev, rank), bf16)]
    others_z = sorted(range(1, chips), key=lambda o: (o == 2, o))
    others_row = list(range(1, rows_count))

    def z_exchange(blocks):
        got = {o: swap(blocks[o - 1], "col", o * CORES) for o in others_z}
        return [got[o] for o in range(1, chips)]

    blocks = [items] + [swap(items, "row", o) for o in others_row]
    send, grad, item_all, item, item_t = call(
        functools.partial(first_peer, rows_count, half),
        [((rank, half), bf16), grad_items, ((rank, items_dev), f32)] + item_pair,
        *blocks, users, preference, flops=work(half),
    )
    recv = swap(send, "col", 1)
    part = half // 2
    kept, grad = call(
        functools.partial(first_own, 0, part, half),
        [((rank, part), f32), grad_items],
        users, preference, item, item_t, grad, flops=work(part),
    )
    piece_outs = [((rank, share), f32)] + [((rank, share), bf16)] * (chips - 1)
    *pieces, grad_b = call(
        functools.partial(first_last, part, half - part, half, share, chips),
        piece_outs + [((rank, items_dev), bf16)],
        users, preference, item, item_t, grad, kept, recv,
        scratch=[pltpu.VMEM((rank, half), f32), pltpu.VMEM((rank, items_dev), f32)],
        flops=work(half - part),
    )
    recvs = z_exchange(pieces[1:])
    grads = [grad_b] + [swap(grad_b, "row", o) for o in others_row]
    new, new_b = call(
        functools.partial(update_share, user_rate, half, share),
        [((rank, share), f32), ((rank, share), bf16)],
        pieces[0], *recvs, users,
    )
    spread = [new_b] + z_exchange([new_b] * (chips - 1))
    item_own, item, item_t, user_half = call(
        functools.partial(second_start, item_rate, rows_count, chips),
        [((rank, block), f32)] + item_pair + [((rank, half), bf16)],
        *grads, item_all, *spread,
    )
    user_peer = swap(user_half, "col", 1)
    first, second = half // 4, half // 2
    kept0, grad = call(
        functools.partial(second_open, 0, first, half),
        [((rank, first), f32), grad_items],
        user_half, preference, item, item_t, flops=work(first),
    )
    send, grad = call(
        functools.partial(second_peer, half),
        [((rank, half), bf16), grad_items],
        user_peer, preference, item, item_t, grad, flops=work(half),
    )
    recv = swap(send, "col", 1)
    kept1, grad = call(
        functools.partial(second_own, first, second, half),
        [((rank, second), f32), grad_items],
        user_half, preference, item, item_t, grad, flops=work(second),
    )
    outs = call(
        functools.partial(second_last, (first, second), half, share, chips, rows_count),
        piece_outs + [((rank, block), f32)] + [((rank, block), bf16)] * (rows_count - 1),
        user_half, preference, item, item_t, grad, kept0, kept1, recv,
        scratch=[pltpu.VMEM((rank, half), f32), pltpu.VMEM((rank, items_dev), f32)],
        flops=work(half - first - second),
    )
    pieces, item_pieces = outs[:chips], outs[chips:]
    recvs = z_exchange(pieces[1:])
    item_recvs = [swap(item_pieces[o], "row", o) for o in others_row]
    (delta_b,) = call(
        functools.partial(update_last, user_rate, half, share),
        [((rank, share), bf16)],
        pieces[0], *recvs, users, new,
    )
    spread = [delta_b] + z_exchange([delta_b] * (chips - 1))
    (new_items,) = call(
        functools.partial(finish_items, item_rate),
        [((rank, block), f32)],
        item_own, item_pieces[0], *item_recvs,
    )
    (delta_half,) = call(functools.partial(gather_half, chips), [((rank, half), bf16)], *spread)
    delta_peer = swap(delta_half, "col", 1)
    (new_users,) = call(
        functools.partial(finish_users, half),
        [((rank, users_dev), f32)],
        users, delta_half, delta_peer,
    )
    return new_users, new_items


def solution(mesh):
    return jax.shard_map(
        body,
        mesh=mesh,
        in_specs=(P("col", "row"), P(None, "row"), P(None, ("col", "row"))),
        out_specs=(P(None, "row"), P(None, ("col", "row"))),
        check_vma=False,
    )
```

```python
import functools
import math

import jax
import jax.numpy as jnp
from jax import lax
from jax.experimental import pallas as pl
from jax.experimental.pallas import tpu as pltpu
from jax.sharding import PartitionSpec as P

CORES = 2
TILE_USERS = 1024
TILE_ITEMS = 512

f32, bf16 = jnp.float32, jnp.bfloat16
VMEM, ANY = pltpu.VMEM, pl.ANY


def swap(block, axis, distance):
    return lax.ppermute(block, axis, [(i, i ^ distance) for i in range(lax.axis_size(axis))])


def tree_sum(terms):
    while len(terms) > 1:
        terms = [terms[i] + terms[i + 1] for i in range(0, len(terms), 2)]
    return terms[0]


def span(index, width):
    return pl.ds(pl.multiple_of(index * width, width), width)


def call(kernel, outs, *args, scratch=(), flops=0, space=VMEM):
    return pl.pallas_call(
        kernel,
        in_specs=[pl.BlockSpec(memory_space=space)] * len(args),
        out_specs=[pl.BlockSpec(memory_space=VMEM)] * len(outs),
        out_shape=[jax.ShapeDtypeStruct(s, d) for s, d in outs],
        scratch_shapes=list(scratch),
        compiler_params=pltpu.CompilerParams(vmem_limit_bytes=24 << 20),
        cost_estimate=pl.CostEstimate(flops=flops, bytes_accessed=1 << 20, transcendentals=0),
    )(*args)


def place():
    col = lax.axis_index("col")
    return lax.axis_index("row"), col // CORES, col % CORES


def group_start(own, near, half):
    _, z, core = place()
    quarter = half // 2
    upper = z // (lax.axis_size("col") // CORES // 2)
    core = core if own else 1 - core
    upper = upper if near else 1 - upper
    return pl.multiple_of(core * half + upper * quarter, quarter)


def row_tiles(items_dev, block, everything):
    if everything:
        tile = min(TILE_ITEMS, items_dev)
        return [(at, tile) for at in range(0, items_dev, tile)]
    row, tiles, size = lax.axis_index("row"), [], 1
    while size * block < items_dev:
        tiles.append((pl.multiple_of(((row // size) ^ 1) * (size * block), size * block), size * block))
        size *= 2
    return tiles


def gradients(tiles, start, width, user_of, item, item_t, labels, grad_item, keep):
    tile_users = min(TILE_USERS, width)
    for at in range(0, width, tile_users):
        here = pl.ds(pl.multiple_of(start + at, tile_users), tile_users)
        user = user_of(at, tile_users)
        total = None
        for first, size in tiles:
            rows = pl.ds(first, size)
            half_scores = jnp.dot(item_t[rows, :], user, preferred_element_type=f32)
            weights = labels[rows, here].astype(f32)
            residual = (jnp.abs(weights) * jnp.tanh(half_scores) - weights).astype(bf16)
            term = jnp.dot(item[:, rows], residual, preferred_element_type=f32)
            total = term if total is None else total + term
            grad_item[:, rows] += lax.dot_general(
                user, residual, (((1,), (1,)), ((), ())), preferred_element_type=f32
            )
        keep(at, tile_users, total)


def put_items(value, item, item_t):
    rounded = value.astype(bf16)
    item[...] = rounded
    item_t[...] = (rounded * jnp.asarray(0.5, bf16)).T


def load_and_own_rows(rows_count, labels_hbm, users_hbm, items_hbm, labels, users, items, grad_user, grad_item, item, item_t, sems):
    row, block = lax.axis_index("row"), items.shape[1]

    def rows_of(o):
        at = span(row ^ o, block)
        return pltpu.make_async_copy(labels_hbm.at[at, :], labels.at[at, :], sems.at[2 + o])

    copies = [
        pltpu.make_async_copy(items_hbm, items, sems.at[0]),
        pltpu.make_async_copy(users_hbm, users, sems.at[1]),
    ] + [rows_of(o) for o in range(rows_count)]
    for copy in copies:
        copy.start()
    copies[0].wait()
    own = span(row, block)
    put_items(items[...], item, item_t)
    grad_item[...] = jnp.zeros_like(grad_item)
    copies[1].wait()
    copies[2].wait()
    width = users.shape[1]
    tile = min(TILE_USERS, width)
    for at in range(0, width, tile):
        here = pl.ds(at, tile)
        user = users[:, here].astype(bf16)
        half_scores = jnp.dot(item_t[...], user, preferred_element_type=f32)
        weights = labels[own, here].astype(f32)
        residual = (jnp.abs(weights) * jnp.tanh(half_scores) - weights).astype(bf16)
        grad_user[:, here] = jnp.dot(item[...], residual, preferred_element_type=f32)
        grad_item[:, own] += lax.dot_general(user, residual, (((1,), (1,)), ((), ())), preferred_element_type=f32)
    for copy in copies[3:]:
        copy.wait()


def first_open(rows_count, half, *refs):
    blocks = refs[:rows_count]
    users, labels, grad_user, grad_in = refs[rows_count : rows_count + 4]
    send, grad_item, item_all, item, item_t = refs[rows_count + 4 :]
    row, block = lax.axis_index("row"), blocks[0].shape[1]
    for o, values in enumerate(blocks):
        item_all[:, span(row ^ o, block)] = values[...]
    put_items(item_all[...], item, item_t)
    first_group(False, False, half, block, users, labels, grad_user, item, item_t, grad_in, send, grad_item)


def first_group(own, near, half, block, users, labels, grad_user, item, item_t, grad_in, out, grad_item):
    start = group_start(own, near, half)
    grad_item[...] = grad_in[...]

    def columns(at, width):
        return pl.ds(pl.multiple_of(start + at, width), width)

    def keep(at, width, total):
        out[:, pl.ds(at, width)] = (total + grad_user[:, columns(at, width)]).astype(out.dtype)

    gradients(
        row_tiles(labels.shape[0], block, False), start, half // 2,
        lambda at, width: users[:, columns(at, width)].astype(bf16),
        item, item_t, labels, grad_item, keep,
    )


def second_group(own, near, half, user_half, labels, item, item_t, grad_in, out, grad_item):
    quarter = half // 2
    start = group_start(own, near, half)
    if grad_in is None:
        grad_item[...] = jnp.zeros_like(grad_item)
    else:
        grad_item[...] = grad_in[...]
    within = lax.rem(start, half)

    def keep(at, width, total):
        out[:, pl.ds(at, width)] = total.astype(out.dtype)

    gradients(
        row_tiles(labels.shape[0], None, True), start, quarter,
        lambda at, width: user_half[:, pl.ds(pl.multiple_of(within + at, width), width)],
        item, item_t, labels, grad_item, keep,
    )


def second_open(near, half, user_half, labels, item, item_t, out, grad_item):
    second_group(True, near, half, user_half, labels, item, item_t, None, out, grad_item)


def combine_far(share, kept, recv, *outs):
    _, z, _ = place()
    far = len(outs)
    for i, out in enumerate(outs):
        at = span(lax.rem(z ^ (far + i), far), share)
        out[...] = (kept[:, at] + recv[:, at].astype(f32)).astype(bf16)


def combine_near(share, kept, recv, own, *outs):
    _, z, _ = place()
    near = len(outs) + 1
    for o in range(near):
        at = span(lax.rem(z ^ o, near), share)
        piece = kept[:, at] + recv[:, at].astype(f32)
        if o == 0:
            own[...] = piece
        else:
            outs[o - 1][...] = piece.astype(bf16)


def combine_near_round(share, kept, recv, grad_item, grad_b, *outs):
    grad_b[...] = grad_item[...].astype(bf16)
    combine_near(share, kept, recv, *outs)


def combine_near_cut(share, rows_count, kept, recv, grad_item, *outs):
    row, block = lax.axis_index("row"), outs[0].shape[1]
    for o in range(rows_count):
        outs[o][...] = grad_item[:, span(row ^ o, block)].astype(outs[o].dtype)
    combine_near(share, kept, recv, *outs[rows_count:])


def share_at(half, share):
    _, z, core = place()
    return pl.ds(pl.multiple_of(core * half + z * share, share), share)


def update_share(rate, half, share, own, *refs):
    recvs, (users, new, new_b) = refs[:-3], refs[-3:]
    grad = tree_sum([own[...]] + [r[...].astype(f32) for r in recvs])
    new[...] = users[:, share_at(half, share)] - rate * grad
    new_b[...] = new[...].astype(bf16)


def update_last(rate, half, share, own, *refs):
    recvs, (users, new, delta_b) = refs[:-3], refs[-3:]
    grad = tree_sum([own[...]] + [r[...].astype(f32) for r in recvs])
    delta_b[...] = (new[...] - rate * grad - users[:, share_at(half, share)]).astype(bf16)


def second_start(rate, rows_count, item_all, *refs):
    grads, (item_own, item, item_t) = refs[:rows_count], refs[rows_count:]
    new = item_all[...] - rate * tree_sum([g[...].astype(f32) for g in grads])
    put_items(new, item, item_t)
    at = span(lax.axis_index("row"), item_own.shape[1])
    item_own[...] = item_all[:, at] - rate * tree_sum([g[:, at].astype(f32) for g in grads])


def assemble(*refs):
    pieces, user_half = refs[:-1], refs[-1]
    _, z, _ = place()
    for o, piece in enumerate(pieces):
        user_half[:, span(z ^ o, piece.shape[1])] = piece[...]


def finish_items(rate, item, own, *refs):
    recvs, out = refs[:-1], refs[-1]
    out[...] = item[...] - rate * tree_sum([own[...]] + [r[...].astype(f32) for r in recvs])


def finish_users(half, users, own, peer, out):
    _, _, core = place()
    mine, other = span(core, half), span(1 - core, half)
    out[:, mine] = users[:, mine] + own[...].astype(f32)
    out[:, other] = users[:, other] + peer[...].astype(f32)


def body(preference, users, items):
    rows_count, cols_count = lax.axis_size("row"), lax.axis_size("col")
    items_dev, users_dev = preference.shape
    rank, block = items.shape
    chips = cols_count // CORES
    half, share = users_dev // CORES, users_dev // cols_count
    quarter = half // 2
    user_rate = 0.5 / math.sqrt(items_dev * cols_count)
    item_rate = 0.5 / math.sqrt(users_dev * rows_count)
    work = 6 * rank * items_dev * quarter
    wide = ((rank, items_dev), f32)
    item_pair = [((rank, items_dev), bf16), ((items_dev, rank), bf16)]
    sent, kept = ((rank, quarter), bf16), ((rank, quarter), f32)
    piece, piece_b = ((rank, share), f32), ((rank, share), bf16)
    half_b = ((rank, half), bf16)
    near, far = list(range(1, chips // 2)), list(range(chips // 2, chips))
    others = list(range(1, rows_count))

    def along_z(block, o):
        return swap(block, "col", o * CORES)

    item_blocks = [swap(items, "row", o) for o in others]
    labels, users_v, items_v, grad_user, grad = call(
        functools.partial(load_and_own_rows, rows_count),
        [(preference.shape, bf16), (users.shape, f32), (items.shape, f32), (users.shape, f32), wide],
        preference, users, items,
        scratch=[VMEM((rank, block), bf16), VMEM((block, rank), bf16), pltpu.SemaphoreType.DMA((rows_count + 2,))],
        space=ANY, flops=work,
    )
    send, grad, item_all, item, item_t = call(
        functools.partial(first_open, rows_count, half), [sent, wide, wide] + item_pair,
        items_v, *item_blocks, users_v, labels, grad_user, grad, flops=work,
    )

    def first(own, near, grad):
        return call(
            functools.partial(first_group, own, near, half, block), [kept if own else sent, wide],
            users_v, labels, grad_user, item, item_t, grad, flops=work,
        )

    recv = swap(send, "col", 1)
    mine, grad = first(True, False, grad)
    far_pieces = call(functools.partial(combine_far, share), [piece_b] * len(far), mine, recv)
    far_got = [along_z(p, o) for p, o in zip(far_pieces, far)]
    *_, grad = lax.optimization_barrier((*far_pieces, grad))
    send, grad = first(False, True, grad)
    recv = swap(send, "col", 1)
    mine, grad = first(True, True, grad)
    grad_b, own, *near_pieces = call(
        functools.partial(combine_near_round, share), [(wide[0], bf16), piece] + [piece_b] * len(near), mine, recv, grad
    )
    near_got = [along_z(p, o) for p, o in zip(near_pieces, near)]
    grads = [grad_b] + [swap(grad_b, "row", o) for o in others]
    new, new_b = call(
        functools.partial(update_share, user_rate, half, share), [piece, piece_b], own, *near_got, *far_got, users_v
    )
    spread = [new_b] + [along_z(new_b, o) for o in near + far]

    item_own, item, item_t = call(
        functools.partial(second_start, item_rate, rows_count), [(items.shape, f32)] + item_pair, item_all, *grads
    )
    (user_half,) = call(assemble, [half_b], *spread)
    user_peer = swap(user_half, "col", 1)
    far_mine, grad = call(
        functools.partial(second_open, False, half), [kept, wide], user_half, labels, item, item_t, flops=work
    )

    def second(own, near, grad):
        return call(
            functools.partial(second_group, own, near, half), [kept if own else sent, wide],
            user_half if own else user_peer, labels, item, item_t, grad, flops=work,
        )

    send, grad = second(False, False, grad)
    far_recv = swap(send, "col", 1)
    send, grad = second(False, True, grad)
    near_recv = swap(send, "col", 1)
    far_pieces = call(functools.partial(combine_far, share), [piece_b] * len(far), far_mine, far_recv)
    far_got = [along_z(p, o) for p, o in zip(far_pieces, far)]
    *_, grad = lax.optimization_barrier((*far_pieces, grad))
    near_mine, grad = second(True, True, grad)
    outs = call(
        functools.partial(combine_near_cut, share, rows_count),
        [(items.shape, f32)] + [(items.shape, bf16)] * len(others) + [piece] + [piece_b] * len(near),
        near_mine, near_recv, grad,
    )
    item_grad, item_pieces, own, near_pieces = outs[0], outs[1:rows_count], outs[rows_count], outs[rows_count + 1 :]
    near_got = [along_z(p, o) for p, o in zip(near_pieces, near)]
    item_got = [swap(p, "row", o) for p, o in zip(item_pieces, others)]
    (delta,) = call(
        functools.partial(update_last, user_rate, half, share), [piece_b], own, *near_got, *far_got, users_v, new
    )
    spread = [delta] + [along_z(delta, o) for o in near + far]
    (new_items,) = call(
        functools.partial(finish_items, item_rate), [(items.shape, f32)], item_own, item_grad, *item_got
    )
    (delta_half,) = call(assemble, [half_b], *spread)
    delta_peer = swap(delta_half, "col", 1)
    (new_users,) = call(functools.partial(finish_users, half), [(users.shape, f32)], users_v, delta_half, delta_peer)
    return new_users, new_items


def solution(mesh):
    return jax.shard_map(
        body,
        mesh=mesh,
        in_specs=(P("col", "row"), P(None, "row"), P(None, ("col", "row"))),
        out_specs=(P(None, "row"), P(None, ("col", "row"))),
        check_vma=False,
    )
```

```python
import functools
import math

import jax
import jax.numpy as jnp
from jax import lax
from jax.experimental import pallas as pl
from jax.experimental.pallas import tpu as pltpu
from jax.sharding import PartitionSpec as P

CORES = 2
TILE_USERS = 1024
TILE_ITEMS = 512

f32, bf16 = jnp.float32, jnp.bfloat16
VMEM, HBM = pltpu.VMEM, pltpu.HBM


def swap(block, axis, distance):
    return lax.ppermute(block, axis, [(i, i ^ distance) for i in range(lax.axis_size(axis))])


def tree_sum(terms):
    while len(terms) > 1:
        terms = [terms[i] + terms[i + 1] for i in range(0, len(terms), 2)]
    return terms[0]


def span(index, width):
    return pl.ds(pl.multiple_of(index * width, width), width)


def call(kernel, outs, *args, scratch=(), flops=0, space=VMEM, grant=24):
    return pl.pallas_call(
        kernel,
        in_specs=[pl.BlockSpec(memory_space=space)] * len(args),
        out_specs=[pl.BlockSpec(memory_space=VMEM)] * len(outs),
        out_shape=[jax.ShapeDtypeStruct(s, d) for s, d in outs],
        scratch_shapes=list(scratch),
        compiler_params=pltpu.CompilerParams(vmem_limit_bytes=grant << 20),
        cost_estimate=pl.CostEstimate(flops=flops, bytes_accessed=1 << 20, transcendentals=0),
    )(*args)


def place():
    col = lax.axis_index("col")
    return lax.axis_index("row"), col // CORES, col % CORES


def group_start(own, near, half):
    _, z, core = place()
    quarter = half // 2
    upper = z // (lax.axis_size("col") // CORES // 2)
    core = core if own else 1 - core
    upper = upper if near else 1 - upper
    return pl.multiple_of(core * half + upper * quarter, quarter)


def row_tiles(items_dev, block, everything):
    if everything:
        tile = min(TILE_ITEMS, items_dev)
        return [(at, tile) for at in range(0, items_dev, tile)]
    row, tiles, size = lax.axis_index("row"), [], 1
    while size * block < items_dev:
        tiles.append((pl.multiple_of(((row // size) ^ 1) * (size * block), size * block), size * block))
        size *= 2
    return tiles


def gradients(tiles, start, width, user_of, item, item_t, labels, grad_item, keep):
    tile_users = min(TILE_USERS, width)
    for at in range(0, width, tile_users):
        here = pl.ds(pl.multiple_of(start + at, tile_users), tile_users)
        user = user_of(at, tile_users)
        total = None
        for first, size in tiles:
            rows = pl.ds(first, size)
            half_scores = jnp.dot(item_t[rows, :], user, preferred_element_type=f32)
            weights = labels[rows, here].astype(f32)
            residual = (jnp.abs(weights) * jnp.tanh(half_scores) - weights).astype(bf16)
            term = jnp.dot(item[:, rows], residual, preferred_element_type=f32)
            total = term if total is None else total + term
            grad_item[:, rows] += lax.dot_general(
                user, residual, (((1,), (1,)), ((), ())), preferred_element_type=f32
            )
        keep(at, tile_users, total)


def put_items(value, item, item_t):
    rounded = value.astype(bf16)
    item[...] = rounded
    item_t[...] = (rounded * jnp.asarray(0.5, bf16)).T


def load_and_own_rows(rows_count, labels_hbm, users_hbm, items_hbm, labels, users, items, grad_user, grad_item, item, item_t, sems):
    row, block = lax.axis_index("row"), items.shape[1]

    def rows_of(o):
        at = span(row ^ o, block)
        return pltpu.make_async_copy(labels_hbm.at[at, :], labels.at[at, :], sems.at[2 + o])

    copies = [
        pltpu.make_async_copy(items_hbm, items, sems.at[0]),
        pltpu.make_async_copy(users_hbm, users, sems.at[1]),
    ] + [rows_of(o) for o in range(rows_count)]
    for copy in copies:
        copy.start()
    copies[0].wait()
    own = span(row, block)
    put_items(items[...], item, item_t)
    grad_item[...] = jnp.zeros_like(grad_item)
    copies[1].wait()
    copies[2].wait()
    width = users.shape[1]
    tile = min(TILE_USERS, width)
    for at in range(0, width, tile):
        here = pl.ds(at, tile)
        user = users[:, here].astype(bf16)
        half_scores = jnp.dot(item_t[...], user, preferred_element_type=f32)
        weights = labels[own, here].astype(f32)
        residual = (jnp.abs(weights) * jnp.tanh(half_scores) - weights).astype(bf16)
        grad_user[:, here] = jnp.dot(item[...], residual, preferred_element_type=f32)
        grad_item[:, own] += lax.dot_general(user, residual, (((1,), (1,)), ((), ())), preferred_element_type=f32)
    for copy in copies[3:]:
        copy.wait()


def first_open(rows_count, half, *refs):
    blocks = refs[:rows_count]
    users, labels, grad_user, grad_in = refs[rows_count : rows_count + 4]
    send, grad_item, item_all, item, item_t = refs[rows_count + 4 :]
    row, block = lax.axis_index("row"), blocks[0].shape[1]
    for o, values in enumerate(blocks):
        item_all[:, span(row ^ o, block)] = values[...]
    put_items(item_all[...], item, item_t)
    first_group(False, False, half, block, users, labels, grad_user, item, item_t, grad_in, send, grad_item)


def first_group(own, near, half, block, users, labels, grad_user, item, item_t, grad_in, out, grad_item):
    start = group_start(own, near, half)
    grad_item[...] = grad_in[...]

    def columns(at, width):
        return pl.ds(pl.multiple_of(start + at, width), width)

    def keep(at, width, total):
        out[:, pl.ds(at, width)] = (total + grad_user[:, columns(at, width)]).astype(out.dtype)

    gradients(
        row_tiles(labels.shape[0], block, False), start, half // 2,
        lambda at, width: users[:, columns(at, width)].astype(bf16),
        item, item_t, labels, grad_item, keep,
    )


def second_group(own, near, half, user_half, labels, item, item_t, grad_in, out, grad_item):
    quarter = half // 2
    start = group_start(own, near, half)
    if grad_in is None:
        grad_item[...] = jnp.zeros_like(grad_item)
    else:
        grad_item[...] = grad_in[...]
    within = lax.rem(start, half)

    def keep(at, width, total):
        out[:, pl.ds(at, width)] = total.astype(out.dtype)

    gradients(
        row_tiles(labels.shape[0], None, True), start, quarter,
        lambda at, width: user_half[:, pl.ds(pl.multiple_of(within + at, width), width)],
        item, item_t, labels, grad_item, keep,
    )


def second_open(near, half, user_half, labels, item, item_t, out, grad_item):
    second_group(True, near, half, user_half, labels, item, item_t, None, out, grad_item)


def combine_far(share, kept, recv, *outs):
    _, z, _ = place()
    far = len(outs)
    for i, out in enumerate(outs):
        at = span(lax.rem(z ^ (far + i), far), share)
        out[...] = (kept[:, at] + recv[:, at].astype(f32)).astype(bf16)


def combine_near(share, kept, recv, own, *outs):
    _, z, _ = place()
    near = len(outs) + 1
    for o in range(near):
        at = span(lax.rem(z ^ o, near), share)
        piece = kept[:, at] + recv[:, at].astype(f32)
        if o == 0:
            own[...] = piece
        else:
            outs[o - 1][...] = piece.astype(bf16)


def combine_near_round(share, kept, recv, grad_item, grad_b, *outs):
    grad_b[...] = grad_item[...].astype(bf16)
    combine_near(share, kept, recv, *outs)


def combine_near_cut(share, rows_count, kept, recv, grad_item, *outs):
    row, block = lax.axis_index("row"), outs[0].shape[1]
    for o in range(rows_count):
        outs[o][...] = grad_item[:, span(row ^ o, block)].astype(outs[o].dtype)
    combine_near(share, kept, recv, *outs[rows_count:])


def share_at(half, share):
    _, z, core = place()
    return pl.ds(pl.multiple_of(core * half + z * share, share), share)


def update_share(rate, half, share, own, *refs):
    recvs, (users, new, new_b) = refs[:-3], refs[-3:]
    grad = tree_sum([own[...]] + [r[...].astype(f32) for r in recvs])
    new[...] = users[:, share_at(half, share)] - rate * grad
    new_b[...] = new[...].astype(bf16)


def update_last(rate, half, share, own, *refs):
    recvs, (users, new, delta_b) = refs[:-3], refs[-3:]
    grad = tree_sum([own[...]] + [r[...].astype(f32) for r in recvs])
    delta_b[...] = (new[...] - rate * grad - users[:, share_at(half, share)]).astype(bf16)


def second_start(rate, rows_count, item_all, *refs):
    grads, (item_own, item, item_t) = refs[:rows_count], refs[rows_count:]
    new = item_all[...] - rate * tree_sum([g[...].astype(f32) for g in grads])
    put_items(new, item, item_t)
    at = span(lax.axis_index("row"), item_own.shape[1])
    item_own[...] = item_all[:, at] - rate * tree_sum([g[:, at].astype(f32) for g in grads])


def assemble(*refs):
    pieces, user_half = refs[:-1], refs[-1]
    _, z, _ = place()
    for o, piece in enumerate(pieces):
        user_half[:, span(z ^ o, piece.shape[1])] = piece[...]


def finish_items(rate, item, own, *refs):
    recvs, out = refs[:-1], refs[-1]
    out[...] = item[...] - rate * tree_sum([own[...]] + [r[...].astype(f32) for r in recvs])


def finish_users(half, users, own, peer, out):
    _, _, core = place()
    mine, other = span(core, half), span(1 - core, half)
    out[:, mine] = users[:, mine] + own[...].astype(f32)
    out[:, other] = users[:, other] + peer[...].astype(f32)


def body(preference, users, items):
    rows_count, cols_count = lax.axis_size("row"), lax.axis_size("col")
    items_dev, users_dev = preference.shape
    rank, block = items.shape
    chips = cols_count // CORES
    half, share = users_dev // CORES, users_dev // cols_count
    quarter = half // 2
    user_rate = 0.5 / math.sqrt(items_dev * cols_count)
    item_rate = 0.5 / math.sqrt(users_dev * rows_count)
    work = 3 * 10**9
    wide = ((rank, items_dev), f32)
    item_pair = [((rank, items_dev), bf16), ((items_dev, rank), bf16)]
    sent, kept = ((rank, quarter), bf16), ((rank, quarter), f32)
    piece, piece_b = ((rank, share), f32), ((rank, share), bf16)
    half_b = ((rank, half), bf16)
    near, far = list(range(1, chips // 2)), list(range(chips // 2, chips))
    others = list(range(1, rows_count))

    def along_z(block, o):
        return swap(block, "col", o * CORES)

    item_blocks = [swap(items, "row", o) for o in others]
    labels, users_v, items_v, grad_user, grad = call(
        functools.partial(load_and_own_rows, rows_count),
        [(preference.shape, bf16), (users.shape, f32), (items.shape, f32), (users.shape, f32), wide],
        preference, users, items,
        scratch=[VMEM((rank, block), bf16), VMEM((block, rank), bf16), pltpu.SemaphoreType.DMA((rows_count + 2,))],
        space=HBM, flops=work, grant=42,
    )
    send, grad, item_all, item, item_t = call(
        functools.partial(first_open, rows_count, half), [sent, wide, wide] + item_pair,
        items_v, *item_blocks, users_v, labels, grad_user, grad, flops=work,
    )

    def first(own, near, grad):
        return call(
            functools.partial(first_group, own, near, half, block), [kept if own else sent, wide],
            users_v, labels, grad_user, item, item_t, grad, flops=work,
        )

    recv = swap(send, "col", 1)
    mine, grad = first(True, False, grad)
    far_pieces = call(functools.partial(combine_far, share), [piece_b] * len(far), mine, recv)
    far_got = [along_z(p, o) for p, o in zip(far_pieces, far)]
    send, grad = first(False, True, grad)
    recv = swap(send, "col", 1)
    mine, grad = first(True, True, grad)
    grad_b, own, *near_pieces = call(
        functools.partial(combine_near_round, share), [(wide[0], bf16), piece] + [piece_b] * len(near), mine, recv, grad
    )
    near_got = [along_z(p, o) for p, o in zip(near_pieces, near)]
    grads = [grad_b] + [swap(grad_b, "row", o) for o in others]
    own, grads[1] = lax.optimization_barrier((own, grads[1]))
    new, new_b = call(
        functools.partial(update_share, user_rate, half, share), [piece, piece_b], own, *near_got, *far_got, users_v
    )
    spread = [new_b] + [along_z(new_b, o) for o in near + far]

    item_own, item, item_t = call(
        functools.partial(second_start, item_rate, rows_count), [(items.shape, f32)] + item_pair, item_all, *grads
    )
    (user_half,) = call(assemble, [half_b], *spread)
    user_peer = swap(user_half, "col", 1)
    far_mine, grad = call(
        functools.partial(second_open, False, half), [kept, wide], user_half, labels, item, item_t, flops=work
    )

    def second(own, near, grad):
        return call(
            functools.partial(second_group, own, near, half), [kept if own else sent, wide],
            user_half if own else user_peer, labels, item, item_t, grad, flops=work,
        )

    send, grad = second(False, False, grad)
    far_recv = swap(send, "col", 1)
    send, grad = second(False, True, grad)
    near_recv = swap(send, "col", 1)
    far_pieces = call(functools.partial(combine_far, share), [piece_b] * len(far), far_mine, far_recv)
    far_got = [along_z(p, o) for p, o in zip(far_pieces, far)]
    near_mine, grad = second(True, True, grad)
    outs = call(
        functools.partial(combine_near_cut, share, rows_count),
        [(items.shape, f32)] + [(items.shape, bf16)] * len(others) + [piece] + [piece_b] * len(near),
        near_mine, near_recv, grad,
    )
    item_grad, item_pieces, own, near_pieces = outs[0], outs[1:rows_count], outs[rows_count], outs[rows_count + 1 :]
    near_got = [along_z(p, o) for p, o in zip(near_pieces, near)]
    item_got = [swap(p, "row", o) for p, o in zip(item_pieces, others)]
    own, *item_got = lax.optimization_barrier((own, *item_got))
    (delta,) = call(
        functools.partial(update_last, user_rate, half, share), [piece_b], own, *near_got, *far_got, users_v, new
    )
    spread = [delta] + [along_z(delta, o) for o in near + far]
    (new_items,) = call(
        functools.partial(finish_items, item_rate), [(items.shape, f32)], item_own, item_grad, *item_got
    )
    (delta_half,) = call(assemble, [half_b], *spread)
    delta_peer = swap(delta_half, "col", 1)
    (new_users,) = call(functools.partial(finish_users, half), [(users.shape, f32)], users_v, delta_half, delta_peer)
    return new_users, new_items


def solution(mesh):
    return jax.shard_map(
        body,
        mesh=mesh,
        in_specs=(P("col", "row"), P(None, "row"), P(None, ("col", "row"))),
        out_specs=(P(None, "row"), P(None, ("col", "row"))),
        check_vma=False,
    )
```

```python
import functools
import math

import jax
import jax.numpy as jnp
from jax import lax
from jax.experimental import pallas as pl
from jax.experimental.pallas import tpu as pltpu
from jax.sharding import PartitionSpec as P

CORES = 2
GROUPS = ((True, True), (False, True), (True, False), (False, False))
TILE_USERS = 1024
TILE_ITEMS = 512

f32, bf16 = jnp.float32, jnp.bfloat16
VMEM, HBM = pltpu.VMEM, pltpu.HBM


def swap(block, axis, distance):
    return lax.ppermute(block, axis, [(i, i ^ distance) for i in range(lax.axis_size(axis))])


def tree_sum(terms):
    while len(terms) > 1:
        terms = [terms[i] + terms[i + 1] for i in range(0, len(terms), 2)]
    return terms[0]


def span(index, width):
    return pl.ds(pl.multiple_of(index * width, width), width)


def call(kernel, outs, *args, scratch=(), flops=0, space=VMEM, grant=24):
    return pl.pallas_call(
        kernel,
        in_specs=[pl.BlockSpec(memory_space=space)] * len(args),
        out_specs=[pl.BlockSpec(memory_space=VMEM)] * len(outs),
        out_shape=[jax.ShapeDtypeStruct(s, d) for s, d in outs],
        scratch_shapes=list(scratch),
        compiler_params=pltpu.CompilerParams(vmem_limit_bytes=grant << 20),
        cost_estimate=pl.CostEstimate(flops=flops, bytes_accessed=1 << 20, transcendentals=0),
    )(*args)


def place():
    col = lax.axis_index("col")
    return lax.axis_index("row"), col // CORES, col % CORES


def bit(level):
    _, z, _ = place()
    return (z >> level) & 1


def group_start(own, keep, half):
    _, _, core = place()
    quarter = half // 2
    core = core if own else 1 - core
    side = bit(0) if keep else 1 - bit(0)
    return pl.multiple_of(core * half + side * quarter, quarter)


def kept_at(half, width):
    _, _, core = place()
    start, level, size = core * half, 0, half // 2
    while size >= width:
        start, level, size = start + bit(level) * size, level + 1, size // 2
    return pl.ds(pl.multiple_of(start, width), width)


def row_tiles(items_dev, block, everything):
    if everything:
        tile = min(TILE_ITEMS, items_dev)
        return [(at, tile) for at in range(0, items_dev, tile)]
    row, tiles, size = lax.axis_index("row"), [], 1
    while size * block < items_dev:
        tiles.append((pl.multiple_of(((row // size) ^ 1) * (size * block), size * block), size * block))
        size *= 2
    return tiles


def gradients(tiles, start, width, user_of, item, item_t, labels, grad_item, keep):
    tile_users = min(TILE_USERS, width)
    for at in range(0, width, tile_users):
        here = pl.ds(pl.multiple_of(start + at, tile_users), tile_users)
        user = user_of(at, tile_users)
        total = None
        for first, size in tiles:
            rows = pl.ds(first, size)
            half_scores = jnp.dot(item_t[rows, :], user, preferred_element_type=f32)
            weights = labels[rows, here].astype(f32)
            residual = (jnp.abs(weights) * jnp.tanh(half_scores) - weights).astype(bf16)
            term = jnp.dot(item[:, rows], residual, preferred_element_type=f32)
            total = term if total is None else total + term
            grad_item[:, rows] += lax.dot_general(
                user, residual, (((1,), (1,)), ((), ())), preferred_element_type=f32
            )
        keep(at, tile_users, total)


def put_items(value, item, item_t):
    rounded = value.astype(bf16)
    item[...] = rounded
    item_t[...] = (rounded * jnp.asarray(0.5, bf16)).T


def load_and_own_rows(rows_count, labels_hbm, users_hbm, items_hbm, labels, users, items, grad_user, grad_item, item, item_t, sems):
    row, block = lax.axis_index("row"), items.shape[1]

    def rows_of(o):
        at = span(row ^ o, block)
        return pltpu.make_async_copy(labels_hbm.at[at, :], labels.at[at, :], sems.at[2 + o])

    copies = [
        pltpu.make_async_copy(items_hbm, items, sems.at[0]),
        pltpu.make_async_copy(users_hbm, users, sems.at[1]),
    ] + [rows_of(o) for o in range(rows_count)]
    for copy in copies:
        copy.start()
    copies[0].wait()
    own = span(row, block)
    put_items(items[...], item, item_t)
    grad_item[...] = jnp.zeros_like(grad_item)
    copies[1].wait()
    copies[2].wait()
    width = users.shape[1]
    tile = min(TILE_USERS, width)
    for at in range(0, width, tile):
        here = pl.ds(at, tile)
        user = users[:, here].astype(bf16)
        half_scores = jnp.dot(item_t[...], user, preferred_element_type=f32)
        weights = labels[own, here].astype(f32)
        residual = (jnp.abs(weights) * jnp.tanh(half_scores) - weights).astype(bf16)
        grad_user[:, here] = jnp.dot(item[...], residual, preferred_element_type=f32)
        grad_item[:, own] += lax.dot_general(user, residual, (((1,), (1,)), ((), ())), preferred_element_type=f32)
    for copy in copies[3:]:
        copy.wait()


def first_open(rows_count, half, *refs):
    blocks = refs[:rows_count]
    users, labels, grad_user, grad_in = refs[rows_count : rows_count + 4]
    send, grad_item, item_all, item, item_t = refs[rows_count + 4 :]
    row, block = lax.axis_index("row"), blocks[0].shape[1]
    for o, values in enumerate(blocks):
        item_all[:, span(row ^ o, block)] = values[...]
    put_items(item_all[...], item, item_t)
    first_group(False, False, half, block, users, labels, grad_user, item, item_t, grad_in, send, grad_item)


def first_group(own, keep_side, half, block, users, labels, grad_user, item, item_t, grad_in, out, grad_item):
    start = group_start(own, keep_side, half)
    grad_item[...] = grad_in[...]

    def columns(at, width):
        return pl.ds(pl.multiple_of(start + at, width), width)

    def keep(at, width, total):
        out[:, pl.ds(at, width)] = (total + grad_user[:, columns(at, width)]).astype(out.dtype)

    gradients(
        row_tiles(labels.shape[0], block, False), start, half // 2,
        lambda at, width: users[:, columns(at, width)].astype(bf16),
        item, item_t, labels, grad_item, keep,
    )


def second_group(own, keep_side, half, user, labels, item, item_t, grad_in, out, grad_item):
    if grad_in is None:
        grad_item[...] = jnp.zeros_like(grad_item)
    else:
        grad_item[...] = grad_in[...]

    def keep(at, width, total):
        out[:, pl.ds(at, width)] = total.astype(out.dtype)

    gradients(
        row_tiles(labels.shape[0], None, True), group_start(own, keep_side, half), half // 2,
        lambda at, width: user[:, pl.ds(at, width)], item, item_t, labels, grad_item, keep,
    )


def second_open(half, user, labels, item, item_t, out, grad_item):
    second_group(True, True, half, user, labels, item, item_t, None, out, grad_item)


def combine(*refs):
    total = refs[0][...]
    for ref in refs[1:-1]:
        total = total + ref[...].astype(f32)
    refs[-1][...] = total.astype(refs[-1].dtype)


def split(level, total, kept, sent):
    width = kept.shape[1]
    kept[...] = total[:, span(bit(level), width)]
    sent[...] = total[:, span(1 - bit(level), width)].astype(bf16)


def join(level, mine, got, out):
    width = mine.shape[1]
    out[:, span(bit(level), width)] = mine[...]
    out[:, span(1 - bit(level), width)] = got[...]


def round_items(grad_item, out):
    out[...] = grad_item[...].astype(bf16)


def cut_items(grad_item, *outs):
    row, block = lax.axis_index("row"), outs[0].shape[1]
    for o, out in enumerate(outs):
        out[...] = grad_item[:, span(row ^ o, block)].astype(out.dtype)


def update_users(rate, half, mine, got, users, new, new_b):
    grad = mine[...].astype(f32) + got[...].astype(f32)
    new[...] = users[:, kept_at(half, mine.shape[1])] - rate * grad
    new_b[...] = new[...].astype(bf16)


def update_last(rate, half, mine, got, users, new, delta):
    grad = mine[...].astype(f32) + got[...].astype(f32)
    delta[...] = (new[...] - rate * grad - users[:, kept_at(half, mine.shape[1])]).astype(bf16)


def second_start(rate, rows_count, item_all, *refs):
    grads, (item_own, item, item_t) = refs[:rows_count], refs[rows_count:]
    new = item_all[...] - rate * tree_sum([g[...].astype(f32) for g in grads])
    put_items(new, item, item_t)
    at = span(lax.axis_index("row"), item_own.shape[1])
    item_own[...] = item_all[:, at] - rate * tree_sum([g[:, at].astype(f32) for g in grads])


def finish_items(rate, item, own, *refs):
    recvs, out = refs[:-1], refs[-1]
    out[...] = item[...] - rate * tree_sum([own[...]] + [r[...].astype(f32) for r in recvs])


def finish_users(half, users, *refs):
    pieces, out = refs[:-1], refs[-1]
    for piece, (own, keep_side) in zip(pieces, GROUPS):
        at = pl.ds(group_start(own, keep_side, half), half // 2)
        out[:, at] = users[:, at] + piece[...].astype(f32)


def body(preference, users, items):
    rows_count, cols_count = lax.axis_size("row"), lax.axis_size("col")
    items_dev, users_dev = preference.shape
    rank, block = items.shape
    chips = cols_count // CORES
    half = users_dev // CORES
    quarter = half // 2
    levels = chips.bit_length() - 1
    user_rate = 0.5 / math.sqrt(items_dev * cols_count)
    item_rate = 0.5 / math.sqrt(users_dev * rows_count)
    work = 3 * 10**9
    wide = ((rank, items_dev), f32)
    item_pair = [((rank, items_dev), bf16), ((items_dev, rank), bf16)]
    sent, kept = ((rank, quarter), bf16), ((rank, quarter), f32)
    others = list(range(1, rows_count))

    def along_z(block, level):
        return swap(block, "col", CORES << level)

    def narrow(mine):
        for level in range(1, levels - 1):
            width = mine.shape[1] // 2
            mine, send = call(functools.partial(split, level), [((rank, width), f32), ((rank, width), bf16)], mine)
            (mine,) = call(combine, [((rank, width), f32)], mine, along_z(send, level))
        return mine

    def widen(block):
        for level in reversed(range(1, levels - 1)):
            outs = [((rank, 2 * block.shape[1]), bf16)]
            (block,) = call(functools.partial(join, level), outs, block, along_z(block, level))
        return block

    def meet(mine, *terms):
        if levels > 2:
            (mine,) = call(combine, [kept], mine, *terms)
            mine, terms = narrow(mine), ()
        (mine,) = call(combine, [(mine.shape, bf16)], mine, *terms)
        return mine, along_z(mine, levels - 1)

    item_blocks = [swap(items, "row", o) for o in others]
    labels, users_v, items_v, grad_user, grad = call(
        functools.partial(load_and_own_rows, rows_count),
        [(preference.shape, bf16), (users.shape, f32), (items.shape, f32), (users.shape, f32), wide],
        preference, users, items,
        scratch=[VMEM((rank, block), bf16), VMEM((block, rank), bf16), pltpu.SemaphoreType.DMA((rows_count + 2,))],
        space=HBM, flops=work, grant=42,
    )
    send, grad, item_all, item, item_t = call(
        functools.partial(first_open, rows_count, half), [sent, wide, wide] + item_pair,
        items_v, *item_blocks, users_v, labels, grad_user, grad, flops=work,
    )

    def first(own, near, grad):
        return call(
            functools.partial(first_group, own, near, half, block), [kept if own else sent, wide],
            users_v, labels, grad_user, item, item_t, grad, flops=work,
        )

    recv = swap(send, "col", 1)
    mine, grad = first(True, False, grad)
    (piece,) = call(combine, [sent], mine, recv)
    near = along_z(piece, 0)
    send, grad = first(False, True, grad)
    recv = swap(send, "col", 1)
    mine, grad = first(True, True, grad)
    (grad_b,) = call(round_items, [(wide[0], bf16)], grad)
    grads = [grad_b] + [swap(grad_b, "row", o) for o in others]
    mine, got = meet(mine, recv, near)
    updated = [(mine.shape, f32), (mine.shape, bf16)]
    new, new_b = call(functools.partial(update_users, user_rate, half), updated, mine, got, users_v)

    def gather(block):
        own_keep = widen(block)
        own_send = along_z(own_keep, 0)
        return own_keep, swap(own_keep, "col", 1), own_send, swap(own_send, "col", 1)

    own_keep, peer_keep, own_send, peer_send = gather(new_b)
    item_own, item, item_t = call(
        functools.partial(second_start, item_rate, rows_count), [(items.shape, f32)] + item_pair, item_all, *grads
    )

    def second(own, keep_side, user, grad):
        return call(
            functools.partial(second_group, own, keep_side, half), [kept if own else sent, wide],
            user, labels, item, item_t, grad, flops=work,
        )

    mine, grad = call(
        functools.partial(second_open, half), [kept, wide], own_keep, labels, item, item_t, flops=work
    )
    send, grad = second(False, True, peer_keep, grad)
    recv = swap(send, "col", 1)
    mine_send, grad = second(True, False, own_send, grad)
    send, grad = second(False, False, peer_send, grad)
    recv_send = swap(send, "col", 1)
    (piece,) = call(combine, [sent], mine_send, recv_send)
    near = along_z(piece, 0)
    item_pieces = call(cut_items, [(items.shape, f32)] + [(items.shape, bf16)] * len(others), grad)
    item_got = [swap(p, "row", o) for p, o in zip(item_pieces[1:], others)]
    mine, got = meet(mine, recv, near)
    got, *item_got = lax.optimization_barrier((got, *item_got))
    (delta,) = call(
        functools.partial(update_last, user_rate, half), [(mine.shape, bf16)], mine, got, users_v, new
    )
    (new_items,) = call(
        functools.partial(finish_items, item_rate), [(items.shape, f32)], item_own, item_pieces[0], *item_got
    )
    (new_users,) = call(functools.partial(finish_users, half), [(users.shape, f32)], users_v, *gather(delta))
    return new_users, new_items


def solution(mesh):
    return jax.shard_map(
        body,
        mesh=mesh,
        in_specs=(P("col", "row"), P(None, "row"), P(None, ("col", "row"))),
        out_specs=(P(None, "row"), P(None, ("col", "row"))),
        check_vma=False,
    )
```

```python
import functools
import math

import jax
import jax.numpy as jnp
from jax import lax
from jax.experimental import pallas as pl
from jax.experimental.pallas import tpu as pltpu
from jax.sharding import PartitionSpec as P

CORES = 2
GROUPS = ((True, True), (False, True), (True, False), (False, False))
TILE_USERS = 1024
TILE_ITEMS = 512

f32, bf16 = jnp.float32, jnp.bfloat16
VMEM, HBM = pltpu.VMEM, pltpu.HBM


def swap(block, axis, distance):
    return lax.ppermute(block, axis, [(i, i ^ distance) for i in range(lax.axis_size(axis))])


def tree_sum(terms):
    while len(terms) > 1:
        terms = [terms[i] + terms[i + 1] for i in range(0, len(terms), 2)]
    return terms[0]


def span(index, width):
    return pl.ds(pl.multiple_of(index * width, width), width)


def call(kernel, outs, *args, scratch=(), flops=0, space=VMEM, grant=24):
    return pl.pallas_call(
        kernel,
        in_specs=[pl.BlockSpec(memory_space=space)] * len(args),
        out_specs=[pl.BlockSpec(memory_space=VMEM)] * len(outs),
        out_shape=[jax.ShapeDtypeStruct(s, d) for s, d in outs],
        scratch_shapes=list(scratch),
        compiler_params=pltpu.CompilerParams(vmem_limit_bytes=grant << 20),
        cost_estimate=pl.CostEstimate(flops=flops, bytes_accessed=1 << 20, transcendentals=0),
    )(*args)


def place():
    col = lax.axis_index("col")
    return lax.axis_index("row"), col // CORES, col % CORES


def bit(level):
    _, z, _ = place()
    return (z >> level) & 1


def group_start(own, keep, half):
    _, _, core = place()
    quarter = half // 2
    core = core if own else 1 - core
    side = bit(0) if keep else 1 - bit(0)
    return pl.multiple_of(core * half + side * quarter, quarter)


def kept_at(half, width):
    _, _, core = place()
    start, level, size = core * half, 0, half // 2
    while size >= width:
        start, level, size = start + bit(level) * size, level + 1, size // 2
    return pl.ds(pl.multiple_of(start, width), width)


def row_tiles(items_dev, block, everything):
    if everything:
        tile = min(TILE_ITEMS, items_dev)
        return [(at, tile) for at in range(0, items_dev, tile)]
    row, tiles, size = lax.axis_index("row"), [], 1
    while size * block < items_dev:
        tiles.append((pl.multiple_of(((row // size) ^ 1) * (size * block), size * block), size * block))
        size *= 2
    return tiles


def gradients(tiles, start, width, user_of, item, item_t, labels, grad_item, keep):
    tile_users = min(TILE_USERS, width)
    for at in range(0, width, tile_users):
        here = pl.ds(pl.multiple_of(start + at, tile_users), tile_users)
        user = user_of(at, tile_users)
        total = None
        for first, size in tiles:
            rows = pl.ds(first, size)
            half_scores = jnp.dot(item_t[rows, :], user, preferred_element_type=f32)
            weights = labels[rows, here].astype(f32)
            residual = (jnp.abs(weights) * jnp.tanh(half_scores) - weights).astype(bf16)
            term = jnp.dot(item[:, rows], residual, preferred_element_type=f32)
            total = term if total is None else total + term
            grad_item[:, rows] += lax.dot_general(
                user, residual, (((1,), (1,)), ((), ())), preferred_element_type=f32
            )
        keep(at, tile_users, total)


def put_items(value, item, item_t):
    rounded = value.astype(bf16)
    item[...] = rounded
    item_t[...] = (rounded * jnp.asarray(0.5, bf16)).T


def hand_on(items, out):
    out[...] = items[...]


def own_rows(labels, users, items, grad_user, grad_item, item, item_t):
    own = span(lax.axis_index("row"), items.shape[1])
    put_items(items[...], item, item_t)
    grad_item[...] = jnp.zeros_like(grad_item)
    width = users.shape[1]
    tile = min(TILE_USERS, width)
    for at in range(0, width, tile):
        here = pl.ds(at, tile)
        user = users[:, here].astype(bf16)
        half_scores = jnp.dot(item_t[...], user, preferred_element_type=f32)
        weights = labels[own, here].astype(f32)
        residual = (jnp.abs(weights) * jnp.tanh(half_scores) - weights).astype(bf16)
        grad_user[:, here] = jnp.dot(item[...], residual, preferred_element_type=f32)
        grad_item[:, own] += lax.dot_general(user, residual, (((1,), (1,)), ((), ())), preferred_element_type=f32)


def first_open(rows_count, half, *refs):
    blocks = refs[:rows_count]
    users, labels, grad_user, grad_in = refs[rows_count : rows_count + 4]
    send, grad_item, item_all, item, item_t = refs[rows_count + 4 :]
    row, block = lax.axis_index("row"), blocks[0].shape[1]
    for o, values in enumerate(blocks):
        item_all[:, span(row ^ o, block)] = values[...]
    put_items(item_all[...], item, item_t)
    first_group(False, False, half, block, users, labels, grad_user, item, item_t, grad_in, send, grad_item)


def first_group(own, keep_side, half, block, users, labels, grad_user, item, item_t, grad_in, out, grad_item):
    start = group_start(own, keep_side, half)
    grad_item[...] = grad_in[...]

    def columns(at, width):
        return pl.ds(pl.multiple_of(start + at, width), width)

    def keep(at, width, total):
        out[:, pl.ds(at, width)] = (total + grad_user[:, columns(at, width)]).astype(out.dtype)

    gradients(
        row_tiles(labels.shape[0], block, False), start, half // 2,
        lambda at, width: users[:, columns(at, width)].astype(bf16),
        item, item_t, labels, grad_item, keep,
    )


def second_group(own, keep_side, half, user, labels, item, item_t, grad_in, out, grad_item):
    if grad_in is None:
        grad_item[...] = jnp.zeros_like(grad_item)
    else:
        grad_item[...] = grad_in[...]

    def keep(at, width, total):
        out[:, pl.ds(at, width)] = total.astype(out.dtype)

    gradients(
        row_tiles(labels.shape[0], None, True), group_start(own, keep_side, half), half // 2,
        lambda at, width: user[:, pl.ds(at, width)], item, item_t, labels, grad_item, keep,
    )


def second_open(half, user, labels, item, item_t, out, grad_item):
    second_group(True, True, half, user, labels, item, item_t, None, out, grad_item)


def combine(*refs):
    total = refs[0][...]
    for ref in refs[1:-1]:
        total = total + ref[...].astype(f32)
    refs[-1][...] = total.astype(refs[-1].dtype)


def split(level, total, kept, sent):
    width = kept.shape[1]
    kept[...] = total[:, span(bit(level), width)]
    sent[...] = total[:, span(1 - bit(level), width)].astype(bf16)


def join(level, mine, got, out):
    width = mine.shape[1]
    out[:, span(bit(level), width)] = mine[...]
    out[:, span(1 - bit(level), width)] = got[...]


def round_items(grad_item, out):
    out[...] = grad_item[...].astype(bf16)


def cut_items(grad_item, *outs):
    row, block = lax.axis_index("row"), outs[0].shape[1]
    for o, out in enumerate(outs):
        out[...] = grad_item[:, span(row ^ o, block)].astype(out.dtype)


def update_users(rate, half, mine, got, users, new, new_b):
    grad = mine[...].astype(f32) + got[...].astype(f32)
    new[...] = users[:, kept_at(half, mine.shape[1])] - rate * grad
    new_b[...] = new[...].astype(bf16)


def update_last(rate, half, mine, got, users, new, delta):
    grad = mine[...].astype(f32) + got[...].astype(f32)
    delta[...] = (new[...] - rate * grad - users[:, kept_at(half, mine.shape[1])]).astype(bf16)


def second_start(rate, rows_count, item_all, *refs):
    grads, (item_own, item, item_t) = refs[:rows_count], refs[rows_count:]
    new = item_all[...] - rate * tree_sum([g[...].astype(f32) for g in grads])
    put_items(new, item, item_t)
    at = span(lax.axis_index("row"), item_own.shape[1])
    item_own[...] = item_all[:, at] - rate * tree_sum([g[:, at].astype(f32) for g in grads])


def finish_items(rate, item, own, *refs):
    recvs, out = refs[:-1], refs[-1]
    out[...] = item[...] - rate * tree_sum([own[...]] + [r[...].astype(f32) for r in recvs])


def finish_users(half, users, *refs):
    pieces, out = refs[:-1], refs[-1]
    for piece, (own, keep_side) in zip(pieces, GROUPS):
        at = pl.ds(group_start(own, keep_side, half), half // 2)
        out[:, at] = users[:, at] + piece[...].astype(f32)


def body(preference, users, items):
    rows_count, cols_count = lax.axis_size("row"), lax.axis_size("col")
    items_dev, users_dev = preference.shape
    rank, block = items.shape
    chips = cols_count // CORES
    half = users_dev // CORES
    quarter = half // 2
    levels = chips.bit_length() - 1
    user_rate = 0.5 / math.sqrt(items_dev * cols_count)
    item_rate = 0.5 / math.sqrt(users_dev * rows_count)
    work = 3 * 10**9
    wide = ((rank, items_dev), f32)
    item_pair = [((rank, items_dev), bf16), ((items_dev, rank), bf16)]
    sent_b, sent, kept = ((rank, quarter), bf16), ((rank, quarter), f32), ((rank, quarter), f32)
    others = list(range(1, rows_count))

    def along_z(block, level):
        return swap(block, "col", CORES << level)

    def narrow(mine):
        for level in range(1, levels - 1):
            width = mine.shape[1] // 2
            mine, send = call(functools.partial(split, level), [((rank, width), f32), ((rank, width), bf16)], mine)
            (mine,) = call(combine, [((rank, width), f32)], mine, along_z(send, level))
        return mine

    def widen(block):
        for level in reversed(range(1, levels - 1)):
            outs = [((rank, 2 * block.shape[1]), bf16)]
            (block,) = call(functools.partial(join, level), outs, block, along_z(block, level))
        return block

    def meet(mine, *terms, behind):
        if levels > 2:
            (mine,) = call(combine, [kept], mine, *terms)
            mine, terms = narrow(mine), ()
        (mine,) = call(combine, [(mine.shape, bf16)], mine, *terms)
        mine, behind = lax.optimization_barrier((mine, behind))
        return mine, along_z(mine, levels - 1), behind

    (items_v,) = call(hand_on, [(items.shape, f32)], items, flops=10 * work)
    item_blocks = [swap(items, "row", o) for o in others]
    labels, users_v = preference, users
    grad_user, grad = call(
        own_rows, [(users.shape, f32), wide], labels, users_v, items_v,
        scratch=[VMEM((rank, block), bf16), VMEM((block, rank), bf16)], flops=work,
    )
    send, grad, item_all, item, item_t = call(
        functools.partial(first_open, rows_count, half), [sent, wide, wide] + item_pair,
        items_v, *item_blocks, users_v, labels, grad_user, grad, flops=work,
    )

    def first(own, near, grad):
        return call(
            functools.partial(first_group, own, near, half, block), [kept if own else sent, wide],
            users_v, labels, grad_user, item, item_t, grad, flops=work,
        )

    recv = swap(send, "col", 1)
    mine, grad = first(True, False, grad)
    (piece,) = call(combine, [sent_b], mine, recv)
    near = along_z(piece, 0)
    piece, grad = lax.optimization_barrier((piece, grad))
    send, grad = first(False, True, grad)
    recv = swap(send, "col", 1)
    mine, grad = first(True, True, grad)
    (grad_b,) = call(round_items, [(wide[0], bf16)], grad)
    mine, got, grad_b = meet(mine, recv, near, behind=grad_b)
    grads = [grad_b] + [swap(grad_b, "row", o) for o in others]
    updated = [(mine.shape, f32), (mine.shape, bf16)]
    new, new_b = call(functools.partial(update_users, user_rate, half), updated, mine, got, users_v)

    own_keep = widen(new_b)
    own_send, peer_keep = along_z(own_keep, 0), swap(own_keep, "col", 1)
    item_own, item, item_t = call(
        functools.partial(second_start, item_rate, rows_count), [(items.shape, f32)] + item_pair, item_all, *grads
    )

    def second(own, keep_side, user, grad):
        return call(
            functools.partial(second_group, own, keep_side, half), [kept if own else sent, wide],
            user, labels, item, item_t, grad, flops=work,
        )

    mine, grad = call(
        functools.partial(second_open, half), [kept, wide], own_keep, labels, item, item_t, flops=work
    )
    send, grad = second(False, True, peer_keep, grad)
    recv = swap(send, "col", 1)
    own_send, grad = lax.optimization_barrier((own_send, grad))
    peer_send = swap(own_send, "col", 1)
    mine_send, grad = second(True, False, own_send, grad)
    send, grad = second(False, False, peer_send, grad)
    recv_send = swap(send, "col", 1)
    (piece,) = call(combine, [sent_b], mine_send, recv_send)
    near = along_z(piece, 0)
    item_pieces = call(cut_items, [(items.shape, f32)] + [(items.shape, bf16)] * len(others), grad)
    mine, got, item_pieces = meet(mine, recv, near, behind=item_pieces)
    item_got = [swap(p, "row", o) for p, o in zip(item_pieces[1:], others)]
    (new_items,) = call(
        functools.partial(finish_items, item_rate), [(items.shape, f32)], item_own, item_pieces[0], *item_got
    )
    got, new_items = lax.optimization_barrier((got, new_items))
    (delta,) = call(
        functools.partial(update_last, user_rate, half), [(mine.shape, bf16)], mine, got, users_v, new
    )
    own_keep = widen(delta)
    own_send = along_z(own_keep, 0)
    pieces = own_keep, swap(own_keep, "col", 1), own_send, swap(own_send, "col", 1)
    (new_users,) = call(functools.partial(finish_users, half), [(users.shape, f32)], users_v, *pieces)
    return new_users, new_items


def solution(mesh):
    return jax.shard_map(
        body,
        mesh=mesh,
        in_specs=(P("col", "row"), P(None, "row"), P(None, ("col", "row"))),
        out_specs=(P(None, "row"), P(None, ("col", "row"))),
        check_vma=False,
    )
```

```python
import functools
import math

import jax
import jax.numpy as jnp
from jax import lax
from jax.experimental import pallas as pl
from jax.experimental.pallas import tpu as pltpu
from jax.sharding import PartitionSpec as P

CORES = 2
GROUPS = ((True, True), (False, True), (True, False), (False, False))
TILE_USERS = 1024
TILE_ITEMS = 1024

f32, bf16 = jnp.float32, jnp.bfloat16
VMEM, HBM = pltpu.VMEM, pltpu.HBM


def swap(block, axis, distance):
    return lax.ppermute(block, axis, [(i, i ^ distance) for i in range(lax.axis_size(axis))])


def tree_sum(terms):
    while len(terms) > 1:
        terms = [terms[i] + terms[i + 1] for i in range(0, len(terms), 2)]
    return terms[0]


def span(index, width):
    return pl.ds(pl.multiple_of(index * width, width), width)


def call(kernel, outs, *args, scratch=(), flops=0, space=VMEM, grant=24):
    return pl.pallas_call(
        kernel,
        in_specs=[pl.BlockSpec(memory_space=space)] * len(args),
        out_specs=[pl.BlockSpec(memory_space=VMEM)] * len(outs),
        out_shape=[jax.ShapeDtypeStruct(s, d) for s, d in outs],
        scratch_shapes=list(scratch),
        compiler_params=pltpu.CompilerParams(vmem_limit_bytes=grant << 20),
        cost_estimate=pl.CostEstimate(flops=flops, bytes_accessed=1 << 20, transcendentals=0),
    )(*args)


def place():
    col = lax.axis_index("col")
    return lax.axis_index("row"), col // CORES, col % CORES


def bit(level):
    _, z, _ = place()
    return (z >> level) & 1


def group_start(own, keep, half):
    _, _, core = place()
    quarter = half // 2
    core = core if own else 1 - core
    side = bit(0) if keep else 1 - bit(0)
    return pl.multiple_of(core * half + side * quarter, quarter)


def kept_at(half, width):
    _, _, core = place()
    start, level, size = core * half, 0, half // 2
    while size >= width:
        start, level, size = start + bit(level) * size, level + 1, size // 2
    return pl.ds(pl.multiple_of(start, width), width)


def row_tiles(items_dev, block, everything):
    if everything:
        tile = min(TILE_ITEMS, items_dev)
        return [(at, tile) for at in range(0, items_dev, tile)]
    row, tiles, size = lax.axis_index("row"), [], 1
    while size * block < items_dev:
        tiles.append((pl.multiple_of(((row // size) ^ 1) * (size * block), size * block), size * block))
        size *= 2
    return tiles


def gradients(tiles, start, width, user_of, item, item_t, labels, grad_item, keep):
    tile_users = min(TILE_USERS, width)
    for at in range(0, width, tile_users):
        here = pl.ds(pl.multiple_of(start + at, tile_users), tile_users)
        user = user_of(at, tile_users)
        total = None
        for first, size in tiles:
            rows = pl.ds(first, size)
            half_scores = jnp.dot(item_t[rows, :], user, preferred_element_type=f32)
            weights = labels[rows, here].astype(f32)
            residual = (jnp.abs(weights) * jnp.tanh(half_scores) - weights).astype(bf16)
            term = jnp.dot(item[:, rows], residual, preferred_element_type=f32)
            total = term if total is None else total + term
            grad_item[:, rows] += lax.dot_general(
                user, residual, (((1,), (1,)), ((), ())), preferred_element_type=f32
            )
        keep(at, tile_users, total)


def put_items(value, item, item_t):
    rounded = value.astype(bf16)
    item[...] = rounded
    item_t[...] = (rounded * jnp.asarray(0.5, bf16)).T


def hand_on(items, out):
    out[...] = items[...]


def own_rows(labels, users, items, grad_user, grad_item, item, item_t):
    own = span(lax.axis_index("row"), items.shape[1])
    put_items(items[...], item, item_t)
    grad_item[...] = jnp.zeros_like(grad_item)
    width = users.shape[1]
    tile = min(TILE_USERS, width)
    for at in range(0, width, tile):
        here = pl.ds(at, tile)
        user = users[:, here].astype(bf16)
        half_scores = jnp.dot(item_t[...], user, preferred_element_type=f32)
        weights = labels[own, here].astype(f32)
        residual = (jnp.abs(weights) * jnp.tanh(half_scores) - weights).astype(bf16)
        grad_user[:, here] = jnp.dot(item[...], residual, preferred_element_type=f32)
        grad_item[:, own] += lax.dot_general(user, residual, (((1,), (1,)), ((), ())), preferred_element_type=f32)


def first_open(rows_count, half, *refs):
    blocks = refs[:rows_count]
    users, labels, grad_user, grad_in = refs[rows_count : rows_count + 4]
    send, grad_item, item_all, item, item_t = refs[rows_count + 4 :]
    row, block = lax.axis_index("row"), blocks[0].shape[1]
    for o, values in enumerate(blocks):
        item_all[:, span(row ^ o, block)] = values[...]
    put_items(item_all[...], item, item_t)
    first_group(False, False, half, block, users, labels, grad_user, item, item_t, grad_in, send, grad_item)


def first_group(own, keep_side, half, block, users, labels, grad_user, item, item_t, grad_in, out, grad_item):
    start = group_start(own, keep_side, half)
    grad_item[...] = grad_in[...]

    def columns(at, width):
        return pl.ds(pl.multiple_of(start + at, width), width)

    def keep(at, width, total):
        out[:, pl.ds(at, width)] = (total + grad_user[:, columns(at, width)]).astype(out.dtype)

    gradients(
        row_tiles(labels.shape[0], block, False), start, half // 2,
        lambda at, width: users[:, columns(at, width)].astype(bf16),
        item, item_t, labels, grad_item, keep,
    )


def second_group(own, keep_side, half, user, labels, item, item_t, grad_in, out, grad_item):
    if grad_in is None:
        grad_item[...] = jnp.zeros_like(grad_item)
    else:
        grad_item[...] = grad_in[...]

    def keep(at, width, total):
        out[:, pl.ds(at, width)] = total.astype(out.dtype)

    gradients(
        row_tiles(labels.shape[0], None, True), group_start(own, keep_side, half), half // 2,
        lambda at, width: user[:, pl.ds(at, width)], item, item_t, labels, grad_item, keep,
    )


def second_open(half, user, labels, item, item_t, out, grad_item):
    second_group(True, True, half, user, labels, item, item_t, None, out, grad_item)


def combine(*refs):
    total = refs[0][...]
    for ref in refs[1:-1]:
        total = total + ref[...].astype(f32)
    refs[-1][...] = total.astype(refs[-1].dtype)


def split(level, total, kept, sent):
    width = kept.shape[1]
    kept[...] = total[:, span(bit(level), width)]
    sent[...] = total[:, span(1 - bit(level), width)].astype(bf16)


def join(level, mine, got, out):
    width = mine.shape[1]
    out[:, span(bit(level), width)] = mine[...]
    out[:, span(1 - bit(level), width)] = got[...]


def round_items(grad_item, out):
    out[...] = grad_item[...].astype(bf16)


def cut_items(grad_item, *outs):
    row, block = lax.axis_index("row"), outs[0].shape[1]
    for o, out in enumerate(outs):
        out[...] = grad_item[:, span(row ^ o, block)].astype(out.dtype)


def update_users(rate, half, mine, got, users, new, new_b):
    grad = mine[...].astype(f32) + got[...].astype(f32)
    new[...] = users[:, kept_at(half, mine.shape[1])] - rate * grad
    new_b[...] = new[...].astype(bf16)


def update_last(rate, half, mine, got, users, new, delta):
    grad = mine[...].astype(f32) + got[...].astype(f32)
    delta[...] = (new[...] - rate * grad - users[:, kept_at(half, mine.shape[1])]).astype(bf16)


def second_start(rate, rows_count, item_all, *refs):
    grads, (item_own, item, item_t) = refs[:rows_count], refs[rows_count:]
    new = item_all[...] - rate * tree_sum([g[...].astype(f32) for g in grads])
    put_items(new, item, item_t)
    at = span(lax.axis_index("row"), item_own.shape[1])
    item_own[...] = item_all[:, at] - rate * tree_sum([g[:, at].astype(f32) for g in grads])


def finish_items(rate, item, own, *refs):
    recvs, out = refs[:-1], refs[-1]
    out[...] = item[...] - rate * tree_sum([own[...]] + [r[...].astype(f32) for r in recvs])


def finish_users(half, users, *refs):
    pieces, out = refs[:-1], refs[-1]
    for piece, (own, keep_side) in zip(pieces, GROUPS):
        at = pl.ds(group_start(own, keep_side, half), half // 2)
        out[:, at] = users[:, at] + piece[...].astype(f32)


def body(preference, users, items):
    rows_count, cols_count = lax.axis_size("row"), lax.axis_size("col")
    items_dev, users_dev = preference.shape
    rank, block = items.shape
    chips = cols_count // CORES
    half = users_dev // CORES
    quarter = half // 2
    levels = chips.bit_length() - 1
    user_rate = 0.5 / math.sqrt(items_dev * cols_count)
    item_rate = 0.5 / math.sqrt(users_dev * rows_count)
    work = 3 * 10**9
    wide = ((rank, items_dev), f32)
    item_pair = [((rank, items_dev), bf16), ((items_dev, rank), bf16)]
    sent_b, sent, kept = ((rank, quarter), bf16), ((rank, quarter), f32), ((rank, quarter), f32)
    others = list(range(1, rows_count))

    def along_z(block, level):
        return swap(block, "col", CORES << level)

    def narrow(mine):
        for level in range(1, levels - 1):
            width = mine.shape[1] // 2
            mine, send = call(functools.partial(split, level), [((rank, width), f32), ((rank, width), bf16)], mine)
            (mine,) = call(combine, [((rank, width), f32)], mine, along_z(send, level))
        return mine

    def widen(block):
        for level in reversed(range(1, levels - 1)):
            outs = [((rank, 2 * block.shape[1]), bf16)]
            (block,) = call(functools.partial(join, level), outs, block, along_z(block, level))
        return block

    def meet(mine, *terms, behind):
        if levels > 2:
            (mine,) = call(combine, [kept], mine, *terms)
            mine, terms = narrow(mine), ()
        (mine,) = call(combine, [(mine.shape, bf16)], mine, *terms)
        mine, behind = lax.optimization_barrier((mine, behind))
        return mine, along_z(mine, levels - 1), behind

    (items_v,) = call(hand_on, [(items.shape, f32)], items, flops=10 * work)
    item_blocks = [swap(items, "row", o) for o in others]
    labels, users_v = preference, users
    grad_user, grad = call(
        own_rows, [(users.shape, f32), wide], labels, users_v, items_v,
        scratch=[VMEM((rank, block), bf16), VMEM((block, rank), bf16)], flops=work,
    )
    send, grad, item_all, item, item_t = call(
        functools.partial(first_open, rows_count, half), [sent, wide, wide] + item_pair,
        items_v, *item_blocks, users_v, labels, grad_user, grad, flops=work,
    )

    def first(own, near, grad):
        return call(
            functools.partial(first_group, own, near, half, block), [kept if own else sent, wide],
            users_v, labels, grad_user, item, item_t, grad, flops=work,
        )

    recv = swap(send, "col", 1)
    mine, grad = first(True, False, grad)
    (piece,) = call(combine, [sent_b], mine, recv)
    near = along_z(piece, 0)
    piece, grad = lax.optimization_barrier((piece, grad))
    send, grad = first(False, True, grad)
    recv = swap(send, "col", 1)
    mine, grad = first(True, True, grad)
    (grad_b,) = call(round_items, [(wide[0], bf16)], grad)
    mine, got, grad_b = meet(mine, recv, near, behind=grad_b)
    grads = [grad_b] + [swap(grad_b, "row", o) for o in others]
    updated = [(mine.shape, f32), (mine.shape, bf16)]
    new, new_b = call(functools.partial(update_users, user_rate, half), updated, mine, got, users_v)

    own_keep = widen(new_b)
    own_send, peer_keep = along_z(own_keep, 0), swap(own_keep, "col", 1)
    item_own, item, item_t = call(
        functools.partial(second_start, item_rate, rows_count), [(items.shape, f32)] + item_pair, item_all, *grads
    )

    def second(own, keep_side, user, grad):
        return call(
            functools.partial(second_group, own, keep_side, half), [kept if own else sent, wide],
            user, labels, item, item_t, grad, flops=work,
        )

    mine, grad = call(
        functools.partial(second_open, half), [kept, wide], own_keep, labels, item, item_t, flops=work
    )
    send, grad = second(False, True, peer_keep, grad)
    recv = swap(send, "col", 1)
    own_send, grad = lax.optimization_barrier((own_send, grad))
    peer_send = swap(own_send, "col", 1)
    mine_send, grad = second(True, False, own_send, grad)
    send, grad = second(False, False, peer_send, grad)
    recv_send = swap(send, "col", 1)
    (piece,) = call(combine, [sent_b], mine_send, recv_send)
    near = along_z(piece, 0)
    item_pieces = call(cut_items, [(items.shape, f32)] + [(items.shape, bf16)] * len(others), grad)
    mine, got, item_pieces = meet(mine, recv, near, behind=item_pieces)
    item_got = [swap(p, "row", o) for p, o in zip(item_pieces[1:], others)]
    got, *item_got = lax.optimization_barrier((got, *item_got))
    (new_items,) = call(
        functools.partial(finish_items, item_rate), [(items.shape, f32)], item_own, item_pieces[0], *item_got
    )
    (delta,) = call(
        functools.partial(update_last, user_rate, half), [(mine.shape, bf16)], mine, got, users_v, new
    )
    own_keep = widen(delta)
    own_send, new_items = lax.optimization_barrier((along_z(own_keep, 0), new_items))
    pieces = own_keep, swap(own_keep, "col", 1), own_send, swap(own_send, "col", 1)
    (new_users,) = call(functools.partial(finish_users, half), [(users.shape, f32)], users_v, *pieces)
    return new_users, new_items


def solution(mesh):
    return jax.shard_map(
        body,
        mesh=mesh,
        in_specs=(P("col", "row"), P(None, "row"), P(None, ("col", "row"))),
        out_specs=(P(None, "row"), P(None, ("col", "row"))),
        check_vma=False,
    )
```
